256 devices in a mesh: ctx: 32 (over x, y, core), tp: 8 (over z).
Axes of the slice: x: 4, y: 4, z: 8, core: 2. Of those that a mesh axis runs over, the one named last changes fastest.
Arguments:
- hidden: bfloat16 [256, 8192], P(None, 'ctx'), may hold values from -6 to 6
- w_query: bfloat16 [8192, 8192], P('ctx', 'tp'), may hold values from -0.0625 to 0.0625
- w_key: bfloat16 [8192, 1024], P('ctx', 'tp'), may hold values from -0.375 to 0.375
- w_value: bfloat16 [8192, 1024], P('ctx', 'tp'), may hold values from -0.0625 to 0.0625
- w_out: bfloat16 [8192, 8192], P('tp', 'ctx'), may hold values from -0.1875 to 0.1875
- key_cache: bfloat16 [131072, 1024], P('ctx', 'tp'), may hold values from -130 to 130
- value_cache: bfloat16 [131072, 1024], P('ctx', 'tp'), may hold values from -6 to 6
- block_count: int32 [32], P('ctx'), may hold values from 512 to 4096, as said below
- positions: int32 [256], replicated, may hold values from 131072 to 131327, as said below
Outputs:
- attended: bfloat16 [256, 8192], P('tp', 'ctx')
The draws below stay inside these ranges and needn't reach their ends.
Inputs may be any that keep to these rules, and one draw needn't show every extreme that they name: `block_count`: at least 512 slots of every block are valid; one block is full in every draw. The query positions are 131072 to 131327, each once, in any order.
All inputs are finite; a program needn't handle non-finite values.
Results may differ from the reference program's by a relative error of at most 0.02.
The reference program's roundings to bfloat16 on the way count: a program that leaves them out, or rounds other values in their place, can miss the bound.
Values may be sent and summed in bfloat16 or wider, within the bound.
No kernel may reach another device: no remote copies, remote signals or barrier semaphores. Data moves between devices by JAX's collectives and lax.ppermute only.
A program may use at most 128 MiB of HBM per device.

```python
import jax
import jax.numpy as jnp
from jax import lax

D = 8192
H = 64
KVH = 8
HD = 128
Q = 256
CTX_DEV = 4096
CONTEXT = 131072
N_CTX = 32


def draw_key_cache(key, part):
    key = jax.random.fold_in(key, 11)
    first = jax.random.fold_in(key, 0)
    values = jnp.clip(3.0 * jax.random.normal(first, (CONTEXT, KVH * HD), jnp.float32), -18.0, 18.0)
    return values.astype(jnp.bfloat16)


def draw_block_count(key, part):
    key = jax.random.fold_in(key, 23)
    first, second = jax.random.split(key)
    counts = jax.random.randint(first, (N_CTX,), CTX_DEV // 8, CTX_DEV + 1)
    chosen = jax.random.randint(second, (), 0, N_CTX)
    return jnp.where(jnp.arange(N_CTX) == chosen, CTX_DEV, counts).astype(jnp.int32)


def draw_positions(key, part):
    key = jax.random.fold_in(key, 37)
    return (CONTEXT + jax.random.permutation(key, Q)).astype(jnp.int32)


def steps_of(key, extent, pieces, low, high):
    factor_of, own = 1.0, jax.random.fold_in(key, 6)
    for dim, shards_of in pieces:
        draws = jnp.exp(jax.random.uniform(jax.random.fold_in(own, dim), (shards_of,), jnp.float32, low / len(pieces), high / len(pieces)))
        factor_of = factor_of * jnp.repeat(draws, extent[dim] // shards_of).reshape([-1 if axis == dim else 1 for axis in range(len(extent))])
    return factor_of


def bell_draw(rng, shape, scale, most, cuts=(), kind=jnp.bfloat16):
    level = steps_of(rng, shape, cuts, -0.22, 0.18) if cuts else 1.0
    entries = jax.random.normal(rng, shape, jnp.float32) * scale * level
    return jnp.minimum(jnp.maximum(entries, -most), most).astype(kind)


def setup_inputs(seed: int = 0) -> dict:
    splits = jax.random.split(jax.random.key(seed), 10)
    return {
        "hidden": bell_draw(splits[0], (Q, D), 1.0, 6.0, ((1, 32),)),
        "w_query": bell_draw(splits[1], (D, H * HD), D ** -0.5, 0.0625, ((0, 32), (1, 8))),
        "w_key": bell_draw(splits[2], (D, KVH * HD), (D // 36) ** -0.5, 0.375, ((0, 32), (1, 8))),
        "w_value": bell_draw(splits[3], (D, KVH * HD), D ** -0.5, 0.0625, ((0, 32), (1, 8))),
        "w_out": bell_draw(splits[4], (H * HD, D), (H * HD // 8) ** -0.5, 0.1875, ((0, 8), (1, 32))),
        "key_cache": draw_key_cache(jax.random.fold_in(splits[9], 71), 0),
        "value_cache": bell_draw(splits[6], (CONTEXT, KVH * HD), 1.0, 6.0, ((0, 32), (1, 8))),
        "block_count": draw_block_count(jax.random.fold_in(splits[9], 71), 0),
        "positions": draw_positions(jax.random.fold_in(splits[9], 71), 0),
    }


def cache_block(queries, key_cache, value_cache, block_count, index):
    start = (index * CTX_DEV).astype(jnp.int32)
    keys = lax.dynamic_slice_in_dim(key_cache, start, CTX_DEV, 0).reshape(CTX_DEV, KVH, HD)
    values = lax.dynamic_slice_in_dim(value_cache, start, CTX_DEV, 0).reshape(CTX_DEV, KVH, HD)
    scores = jnp.einsum('qkgd,tkd->kgqt', queries.astype(jnp.float32), keys.astype(jnp.float32))
    valid = jnp.arange(CTX_DEV, dtype=jnp.int32)[None, None, None, :] < block_count[index]
    largest = jnp.max(jnp.where(valid, scores, -jnp.inf), axis=-1)
    weights = jnp.where(valid, jnp.exp(scores - largest[..., None]), 0.0)
    total = jnp.sum(weights, axis=-1)
    rounded = weights.astype(jnp.bfloat16)
    summed = jnp.einsum('kgqt,tkd->kgqd', rounded.astype(jnp.float32), values.astype(jnp.float32))
    return largest, total, summed


def reference(hidden, w_query, w_key, w_value, w_out, key_cache, value_cache, block_count, positions):
    group = H // KVH
    query_full = jnp.dot(hidden, w_query, preferred_element_type=jnp.float32)
    queries = (query_full * (HD ** -0.5)).astype(jnp.bfloat16).reshape(Q, KVH, group, HD)
    new_keys = jnp.dot(hidden, w_key, preferred_element_type=jnp.float32).astype(jnp.bfloat16).reshape(Q, KVH, HD)
    new_values = jnp.dot(hidden, w_value, preferred_element_type=jnp.float32).astype(jnp.bfloat16).reshape(Q, KVH, HD)
    tops, totals, sums = lax.map(
        lambda index: cache_block(queries, key_cache, value_cache, block_count, index),
        jnp.arange(N_CTX, dtype=jnp.int32))
    largest = jnp.max(tops, axis=0)
    factor = jnp.exp(tops - largest[None])
    total = jnp.sum(totals * factor, axis=0)
    summed = jnp.sum(sums * factor[..., None], axis=0)
    own_scores = jnp.einsum('qkgd,jkd->kgqj', queries.astype(jnp.float32), new_keys.astype(jnp.float32))
    visible = (positions[None, :] <= positions[:, None])[None, None]
    own_top = jnp.max(jnp.where(visible, own_scores, -jnp.inf), axis=-1)
    own_weights = jnp.where(visible, jnp.exp(own_scores - own_top[..., None]), 0.0)
    own_total = jnp.sum(own_weights, axis=-1)
    own_sum = jnp.einsum('kgqj,jkd->kgqd', own_weights.astype(jnp.bfloat16).astype(jnp.float32), new_values.astype(jnp.float32))
    both = jnp.maximum(largest, own_top)
    first = jnp.exp(largest - both)
    second = jnp.exp(own_top - both)
    total = total * first + own_total * second
    summed = summed * first[..., None] + own_sum * second[..., None]
    context = (summed / total[..., None]).transpose(2, 0, 1, 3).reshape(Q, H * HD).astype(jnp.bfloat16)
    return jnp.dot(context, w_out, preferred_element_type=jnp.float32).astype(jnp.bfloat16)
```

```python
import functools

import jax
import jax.numpy as jnp
from jax import lax
from jax.experimental import pallas as pl
from jax.experimental.pallas import tpu as pltpu
from jax.sharding import PartitionSpec as P

H = 64
KVH = 8
HD = 128
SPAN = 2048
STEP = 512
LOG2E = 1.4426950408889634
LARGE = 2.0**100
SMALL = 2.0**-60
ROWS_BY_ROWS = (((1,), (1,)), ((), ()))
VMEM = pl.BlockSpec(memory_space=pltpu.VMEM)
SMEM = pl.BlockSpec(memory_space=pltpu.SMEM)
KERNEL = pltpu.CompilerParams(vmem_limit_bytes=40 * 2**20)


def sum_kernel(width, pieces, queries, other):
    total = jnp.sum(pieces[...], axis=0)
    rows = (total[:, :width] * HD ** (-0.5)).astype(jnp.bfloat16)
    for place in range(queries.shape[0]):
        queries[place] = rows
    other[...] = total[:, width:].astype(jnp.bfloat16)


def three_parts(value):
    high = value.astype(jnp.bfloat16).astype(jnp.float32)
    rest = value - high
    middle = rest.astype(jnp.bfloat16).astype(jnp.float32)
    return (high, middle, rest - middle)


def attend_kernel(
    heads, count, queries, keys0, values0, keys1, values1, new_keys, new_values,
    row_positions, key_positions, out, wide, reference, total, summed,
):
    rows = queries.shape[0]
    blocks = ((keys0, values0), (keys1, values1))
    lane = lax.broadcasted_iota(jnp.int32, (rows, HD), 1)
    visible = key_positions[...] <= row_positions[...]

    def own_scores(head):
        scores = lax.dot_general(
            queries[:, head * HD : (head + 1) * HD], new_keys[...], ROWS_BY_ROWS,
            preferred_element_type=jnp.float32,
        )
        return jnp.where(visible, scores, -jnp.inf)

    for head in range(heads):
        at = slice(head * rows, (head + 1) * rows)
        query = queries[:, head * HD : (head + 1) * HD]
        sample = lax.dot_general(
            query, keys0[:256, :], ROWS_BY_ROWS, preferred_element_type=jnp.float32
        )
        scores = own_scores(head)
        top = jnp.maximum(
            jnp.max(sample, axis=1, keepdims=True), jnp.max(scores, axis=1, keepdims=True)
        )
        level = jnp.broadcast_to(top, (rows, HD)).astype(jnp.bfloat16).astype(jnp.float32)
        wide[at, :HD] = query
        wide[at, HD:] = jnp.where(lane == 0, -level, jnp.where(lane == 1, 1.0, 0.0)).astype(
            jnp.bfloat16
        )
        weights = jnp.exp2((scores - level) * LOG2E)
        reference[at] = level
        total[at] = jnp.broadcast_to(jnp.sum(weights, axis=1, keepdims=True), (rows, HD))
        summed[at] = jnp.dot(
            weights.astype(jnp.bfloat16), new_values[...], preferred_element_type=jnp.float32
        )

    span_lane = lax.broadcasted_iota(jnp.int32, (SPAN, HD), 1)
    span_row = lax.broadcasted_iota(jnp.int32, (SPAN, HD), 0)

    for which, (keys, values) in enumerate(blocks):
        limit = count[which]

        def read_span(step, carry, keys=keys, values=values, limit=limit):
            start = pl.multiple_of(step * SPAN, SPAN)
            bias = jnp.where(span_row + start < limit, 0.0, -1e30)
            extra = jnp.where(span_lane == 0, 1.0, jnp.where(span_lane == 1, bias, 0.0))
            key = jnp.concatenate(
                [keys[pl.ds(start, SPAN), :], extra.astype(jnp.bfloat16)], axis=1
            )
            value = values[pl.ds(start, SPAN), :]
            for head in range(heads):
                at = slice(head * rows, (head + 1) * rows)
                scores = lax.dot_general(
                    wide[at], key, ROWS_BY_ROWS, preferred_element_type=jnp.float32
                )
                weights = jnp.exp2(scores * LOG2E)
                total[at] = total[at] + jnp.sum(weights, axis=1, keepdims=True)
                summed[at] = summed[at] + jnp.dot(
                    weights.astype(jnp.bfloat16), value, preferred_element_type=jnp.float32
                )
            return carry

        lax.fori_loop(0, (limit + SPAN - 1) // SPAN, read_span, 0)

    in_range = jnp.logical_and(jnp.max(total[...]) < LARGE, jnp.min(total[...]) > SMALL)

    @pl.when(jnp.logical_not(in_range))
    def _():
        reference[...] = jnp.full_like(reference, -jnp.inf)
        total[...] = jnp.zeros_like(total)
        summed[...] = jnp.zeros_like(summed)

        def update(at, scores, value):
            before = reference[at]
            now = jnp.maximum(before, jnp.max(scores, axis=1, keepdims=True))
            keep = jnp.exp(before - now)
            weights = jnp.exp(scores - now[:, :1])
            total[at] = total[at] * keep + jnp.sum(weights, axis=1, keepdims=True)
            summed[at] = summed[at] * keep + jnp.dot(
                weights.astype(jnp.bfloat16), value, preferred_element_type=jnp.float32
            )
            reference[at] = now

        for which, (keys, values) in enumerate(blocks):
            limit = count[which]

            def read_step(step, carry, keys=keys, values=values, limit=limit):
                start = pl.multiple_of(step * STEP, STEP)
                valid = start + lax.broadcasted_iota(jnp.int32, (1, STEP), 1) < limit
                key = keys[pl.ds(start, STEP), :]
                value = values[pl.ds(start, STEP), :]
                for head in range(heads):
                    scores = lax.dot_general(
                        queries[:, head * HD : (head + 1) * HD], key, ROWS_BY_ROWS,
                        preferred_element_type=jnp.float32,
                    )
                    update(
                        slice(head * rows, (head + 1) * rows),
                        jnp.where(valid, scores, -jnp.inf),
                        value,
                    )
                return carry

            lax.fori_loop(0, (limit + STEP - 1) // STEP, read_step, 0)
        for head in range(heads):
            update(slice(head * rows, (head + 1) * rows), own_scores(head), new_values[...])

    statistics = jnp.zeros((rows, HD), jnp.float32)
    for head in range(heads):
        at = slice(head * rows, (head + 1) * rows)
        out[:, head * HD : (head + 1) * HD] = summed[at].astype(jnp.bfloat16)
        parts = three_parts(reference[at]) + three_parts(total[at])
        for place, part in enumerate(parts):
            statistics = jnp.where(lane == 8 * head + place, part, statistics)
    out[:, heads * HD :] = statistics.astype(jnp.bfloat16)


def combine_kernel(heads, pieces, out):
    sources, rows, _ = pieces.shape
    width = heads * HD
    statistics = pieces[:, :, width:].reshape(sources * rows, HD)
    place = lax.broadcasted_iota(jnp.int32, (HD, width), 0)
    column = lax.broadcasted_iota(jnp.int32, (HD, width), 1)
    own = place // 8 == column // HD
    pick_top = jnp.where(own & (place % 8 < 3), 1.0, 0.0).astype(jnp.bfloat16)
    pick_total = jnp.where(own & (place % 8 >= 3) & (place % 8 < 6), 1.0, 0.0)
    tops = jnp.dot(statistics, pick_top, preferred_element_type=jnp.float32)
    totals = jnp.dot(
        statistics, pick_total.astype(jnp.bfloat16), preferred_element_type=jnp.float32
    )
    tops = tops.reshape(sources, rows, width)
    totals = totals.reshape(sources, rows, width)
    scale = jnp.exp(tops - jnp.max(tops, axis=0, keepdims=True))
    summed = jnp.sum(scale * pieces[:, :, :width].astype(jnp.float32), axis=0)
    context = (summed / jnp.sum(scale * totals, axis=0)).astype(jnp.bfloat16)
    for target in range(out.shape[0]):
        out[target] = context


def on_device(
    shards, hidden, w_query, w_key, w_value, w_out, key_cache, value_cache, block_count, positions
):
    query_count = hidden.shape[0]
    chips = shards // 2
    rows = query_count // chips
    half = w_query.shape[1] // 2
    heads = half // HD
    place = lax.axis_index("ctx")
    chip = place // 2
    first = place % 2 == 0
    swap = [(index, index ^ 1) for index in range(shards)]
    same_core = [[2 * index + core for index in range(chips)] for core in range(2)]

    def exchange(array):
        return lax.all_to_all(array, "ctx", 0, 0, axis_index_groups=same_core)

    low, high = w_query[:, :half], w_query[:, half:]
    own_columns = jnp.concatenate(
        [jnp.where(first, low, high), jnp.where(first, w_key, w_value)], axis=1
    )
    sent_columns = jnp.concatenate(
        [jnp.where(first, high, low), jnp.where(first, w_value, w_key)], axis=1
    )
    hidden_other = lax.ppermute(hidden, "ctx", swap)
    columns_other = lax.ppermute(sent_columns, "ctx", swap)
    keys_other = lax.ppermute(key_cache, "ctx", swap)
    values_other = lax.ppermute(value_cache, "ctx", swap)
    count_other = lax.ppermute(block_count, "ctx", swap)
    partial = jnp.dot(hidden, own_columns, preferred_element_type=jnp.float32) + jnp.dot(
        hidden_other, columns_other, preferred_element_type=jnp.float32
    )
    pieces = exchange(partial.reshape(chips, rows, half + HD))
    query_rows, new_own = pl.pallas_call(
        functools.partial(sum_kernel, half),
        out_shape=(
            jax.ShapeDtypeStruct((chips, rows, half), jnp.bfloat16),
            jax.ShapeDtypeStruct((rows, HD), jnp.bfloat16),
        ),
        in_specs=[VMEM],
        out_specs=(VMEM, VMEM),
        compiler_params=KERNEL,
    )(pieces)
    new_other = lax.ppermute(new_own, "ctx", swap)
    queries = exchange(query_rows).reshape(query_count, half)
    padding = ((0, HD - rows), (0, 0))
    new_keys = jnp.pad(jnp.where(first, new_own, new_other), padding)
    new_values = jnp.pad(jnp.where(first, new_other, new_own), padding)
    key_positions = jnp.pad(
        lax.dynamic_slice_in_dim(positions, chip * rows, rows, 0),
        (0, HD - rows),
        constant_values=jnp.iinfo(jnp.int32).max,
    )[None, :]
    local = pl.pallas_call(
        functools.partial(attend_kernel, heads),
        out_shape=jax.ShapeDtypeStruct((query_count, half + HD), jnp.bfloat16),
        in_specs=[SMEM] + [VMEM] * 9,
        out_specs=VMEM,
        scratch_shapes=[
            pltpu.VMEM((heads * query_count, 2 * HD), jnp.bfloat16),
            pltpu.VMEM((heads * query_count, HD), jnp.float32),
            pltpu.VMEM((heads * query_count, HD), jnp.float32),
            pltpu.VMEM((heads * query_count, HD), jnp.float32),
        ],
        compiler_params=KERNEL,
    )(
        jnp.concatenate([block_count, count_other]),
        queries,
        key_cache,
        value_cache,
        keys_other,
        values_other,
        new_keys,
        new_values,
        positions[:, None],
        key_positions,
    )
    groups = exchange(local.reshape(chips, rows, half + HD))
    context_rows = pl.pallas_call(
        functools.partial(combine_kernel, heads),
        out_shape=jax.ShapeDtypeStruct((chips, rows, half), jnp.bfloat16),
        in_specs=[VMEM],
        out_specs=VMEM,
        compiler_params=KERNEL,
    )(groups)
    context = exchange(context_rows).reshape(query_count, half)
    context_other = lax.ppermute(context, "ctx", swap)
    start = (place % 2) * half
    out_own = lax.dynamic_slice_in_dim(w_out, start, half, 0)
    out_other = lax.dynamic_slice_in_dim(w_out, half - start, half, 0)
    attended = jnp.dot(context, out_own, preferred_element_type=jnp.float32) + jnp.dot(
        context_other, out_other, preferred_element_type=jnp.float32
    )
    parts = lax.axis_size("tp")
    attended = attended.astype(jnp.bfloat16).reshape(parts, query_count // parts, -1)
    received = lax.all_to_all(attended, "tp", 0, 0)
    return jnp.sum(received.astype(jnp.float32), axis=0).astype(jnp.bfloat16)


def solution(mesh):
    return jax.shard_map(
        functools.partial(on_device, mesh.shape["ctx"]),
        mesh=mesh,
        in_specs=(
            P(None, "ctx"),
            P("ctx", "tp"),
            P("ctx", "tp"),
            P("ctx", "tp"),
            P("tp", "ctx"),
            P("ctx", "tp"),
            P("ctx", "tp"),
            P("ctx"),
            P(),
        ),
        out_specs=P("tp", "ctx"),
        check_vma=False,
    )
```

```python
import functools

import jax
import jax.numpy as jnp
from jax import lax
from jax.experimental import pallas as pl
from jax.experimental.pallas import tpu as pltpu
from jax.sharding import PartitionSpec as P

H = 64
KVH = 8
HD = 128
SPAN = 2048
CHUNK = 1024
STEP = 512
LOG2E = 1.4426950408889634
LARGE = 2.0**100
SMALL = 2.0**-60
ROWS_BY_ROWS = (((1,), (1,)), ((), ()))
VMEM = pl.BlockSpec(memory_space=pltpu.VMEM)
SMEM = pl.BlockSpec(memory_space=pltpu.SMEM)
HBM = pl.BlockSpec(memory_space=pltpu.HBM)
KERNEL = pltpu.CompilerParams(vmem_limit_bytes=32 * 2**20)


def core_of():
    return lax.rem(lax.axis_index("ctx"), 2)


def project_kernel(packed, hidden, query, key, value, out, sample):
    sample[...] = packed[:HD, -HD:]
    core = core_of()
    chips, rows, _ = out.shape
    width = query.shape[1]
    half = width // 2
    depth = hidden.shape[1]
    starts = [depth + core * half, depth + width + core * HD]
    own = [
        packed[:, pl.ds(pl.multiple_of(start, HD), size)]
        for start, size in zip(starts, (half, HD))
    ]

    def product(one, two):
        return (
            jnp.dot(packed[:, :depth], one, preferred_element_type=jnp.float32)
            + jnp.dot(hidden[...], two, preferred_element_type=jnp.float32)
        ).reshape(chips, rows, -1)

    columns = pl.ds(pl.multiple_of(core * half, half), half)
    out[:, :, :half] = product(own[0], query[:, columns])
    for index, weights in enumerate((key, value)):

        @pl.when(core == index)
        def _(weights=weights):
            out[:, :, half:] = product(own[1], weights[...])


def sum_kernel(width, pieces, queries, other):
    total = jnp.sum(pieces[...], axis=0)
    rows = (total[:, :width] * HD ** (-0.5)).astype(jnp.bfloat16)
    for place in range(queries.shape[0]):
        queries[place] = rows
    other[...] = total[:, width:].astype(jnp.bfloat16)


def three_parts(value):
    high = value.astype(jnp.bfloat16).astype(jnp.float32)
    rest = value - high
    middle = rest.astype(jnp.bfloat16).astype(jnp.float32)
    return (high, middle, rest - middle)


def attend_kernel(
    heads, count0, count1, queries, sample_keys, keys0, values0, keys1, values1, new_own,
    new_other, positions, out, keys, values, new_keys, new_values, stacked, reference, total,
    summed, arrivals,
):
    rows = queries.shape[0]
    block = keys0.shape[0]
    fetches = [
        pltpu.make_async_copy(
            source, target.at[pl.ds(index // 2 * block, block)], arrivals.at[index]
        )
        for index, (source, target) in enumerate(
            ((keys0, keys), (values0, values), (keys1, keys), (values1, values))
        )
    ]
    for fetch in fetches[:2]:
        fetch.start()
    lane = lax.broadcasted_iota(jnp.int32, (rows, HD), 1)
    count = new_own.shape[0]
    first = lax.axis_index("ctx") // 2 * count
    offset = lax.rem(first, HD)
    row_positions = jnp.transpose(jnp.broadcast_to(positions[...], (HD, rows)))
    key_positions = positions[:, pl.ds(pl.multiple_of(first - offset, HD), HD)]
    visible = (key_positions <= row_positions) & (lane >= offset) & (lane < offset + count)
    new_keys[...] = jnp.zeros_like(new_keys)
    new_values[...] = jnp.zeros_like(new_values)
    new_at = pl.ds(pl.multiple_of(offset, count), count)
    for index, pair in enumerate(((new_own, new_other), (new_other, new_own))):

        @pl.when(core_of() == index)
        def _(pair=pair):
            new_keys[new_at] = pair[0][...]
            new_values[new_at] = pair[1][...]

    def score(query, key):
        return lax.dot_general(
            query, key, ROWS_BY_ROWS, preferred_element_type=jnp.float32
        )

    sample = jnp.concatenate([sample_keys[...], new_keys[...]], axis=0)
    for head in range(heads):
        at = slice(head * rows, (head + 1) * rows)
        query = queries[:, head * HD : (head + 1) * HD]
        scores = score(query, sample)
        own = jnp.where(visible, scores[:, HD:], -jnp.inf)
        top = jnp.max(jnp.maximum(scores[:, :HD], own), axis=1, keepdims=True)
        level = jnp.broadcast_to(top, (rows, HD)).astype(jnp.bfloat16).astype(jnp.float32)
        stacked[at, :HD] = query
        stacked[at, HD:] = jnp.where(
            lane == 0, -level, jnp.where(lane == 1, 1.0, 0.0)
        ).astype(jnp.bfloat16)
        weights = jnp.exp2((own - level) * LOG2E)
        reference[at] = level
        total[at] = jnp.broadcast_to(jnp.sum(weights, axis=1, keepdims=True), (rows, HD))
        summed[at] = jnp.dot(
            weights.astype(jnp.bfloat16), new_values[...], preferred_element_type=jnp.float32
        )

    for fetch in fetches[2:]:
        fetch.start()
    span_lane = lax.broadcasted_iota(jnp.int32, (SPAN, HD), 1)

    def read_block(which, carry):
        for near in range(2):

            @pl.when(which == near)
            def _(near=near):
                fetches[2 * near].wait()
                fetches[2 * near + 1].wait()

        base = which * block
        limit = jnp.where(which == 0, count0[0], count1[0])

        def read_span(step, carry):
            start = pl.multiple_of(base + step * SPAN, SPAN)
            value = values[pl.ds(start, SPAN), :]
            place = step * SPAN + lax.broadcasted_iota(jnp.int32, (SPAN, HD), 0)
            bias = jnp.where(place < limit, 0.0, -1e30)
            extra = jnp.where(span_lane == 0, 1.0, jnp.where(span_lane == 1, bias, 0.0))
            key = jnp.concatenate(
                [keys[pl.ds(start, SPAN), :], extra.astype(jnp.bfloat16)], axis=1
            )
            for first_row in range(0, heads * rows, CHUNK):
                at = slice(first_row, first_row + CHUNK)
                scores = score(stacked[at], key)
                weights = jnp.exp2(scores * LOG2E)
                total[at] = total[at] + jnp.sum(weights, axis=1, keepdims=True)
                summed[at] = summed[at] + jnp.dot(
                    weights.astype(jnp.bfloat16), value, preferred_element_type=jnp.float32
                )
            return carry

        return lax.fori_loop(0, (limit + SPAN - 1) // SPAN, read_span, carry)

    lax.fori_loop(0, 2, read_block, 0)
    in_range = jnp.logical_and(jnp.max(total[...]) < LARGE, jnp.min(total[...]) > SMALL)

    @pl.when(jnp.logical_not(in_range))
    def _():
        reference[...] = jnp.full_like(reference, -jnp.inf)
        total[...] = jnp.zeros_like(total)
        summed[...] = jnp.zeros_like(summed)

        def update(at, scores, value):
            before = reference[at]
            now = jnp.maximum(before, jnp.max(scores, axis=1, keepdims=True))
            keep = jnp.exp(before - now)
            weights = jnp.exp(scores - now[:, :1])
            total[at] = total[at] * keep + jnp.sum(weights, axis=1, keepdims=True)
            summed[at] = summed[at] * keep + jnp.dot(
                weights.astype(jnp.bfloat16), value, preferred_element_type=jnp.float32
            )
            reference[at] = now

        def query_of(head):
            return queries[:, head * HD : (head + 1) * HD]

        def read_again(which, carry):
            base = which * block
            limit = jnp.where(which == 0, count0[0], count1[0])

            def read_step(step, carry):
                start = pl.multiple_of(base + step * STEP, STEP)
                place = step * STEP + lax.broadcasted_iota(jnp.int32, (1, STEP), 1)
                key = keys[pl.ds(start, STEP), :]
                value = values[pl.ds(start, STEP), :]
                for head in range(heads):
                    scores = jnp.where(place < limit, score(query_of(head), key), -jnp.inf)
                    update(slice(head * rows, (head + 1) * rows), scores, value)
                return carry

            return lax.fori_loop(0, (limit + STEP - 1) // STEP, read_step, carry)

        lax.fori_loop(0, 2, read_again, 0)
        for head in range(heads):
            scores = jnp.where(visible, score(query_of(head), new_keys[...]), -jnp.inf)
            update(slice(head * rows, (head + 1) * rows), scores, new_values[...])

    statistics = jnp.zeros((rows, HD), jnp.float32)
    for head in range(heads):
        at = slice(head * rows, (head + 1) * rows)
        out[:, head * HD : (head + 1) * HD] = summed[at].astype(jnp.bfloat16)
        parts = three_parts(reference[at]) + three_parts(total[at])
        for place, part in enumerate(parts):
            statistics = jnp.where(lane == 8 * head + place, part, statistics)
    out[:, heads * HD :] = statistics.astype(jnp.bfloat16)


def combine_kernel(heads, pieces, out):
    sources, rows, _ = pieces.shape
    width = heads * HD
    statistics = pieces[:, :, width:].reshape(sources * rows, HD)
    place = lax.broadcasted_iota(jnp.int32, (HD, width), 0)
    column = lax.broadcasted_iota(jnp.int32, (HD, width), 1)
    own = place // 8 == column // HD
    pick_top = jnp.where(own & (place % 8 < 3), 1.0, 0.0).astype(jnp.bfloat16)
    pick_total = jnp.where(own & (place % 8 >= 3) & (place % 8 < 6), 1.0, 0.0)
    tops = jnp.dot(statistics, pick_top, preferred_element_type=jnp.float32)
    totals = jnp.dot(
        statistics, pick_total.astype(jnp.bfloat16), preferred_element_type=jnp.float32
    )
    tops = tops.reshape(sources, rows, width)
    totals = totals.reshape(sources, rows, width)
    scale = jnp.exp(tops - jnp.max(tops, axis=0, keepdims=True))
    summed = jnp.sum(scale * pieces[:, :, :width].astype(jnp.float32), axis=0)
    context = (summed / jnp.sum(scale * totals, axis=0)).astype(jnp.bfloat16)
    for target in range(out.shape[0]):
        out[target] = context


def on_device(
    shards, hidden, w_query, w_key, w_value, w_out, key_cache, value_cache, block_count, positions
):
    query_count = hidden.shape[0]
    chips = shards // 2
    rows = query_count // chips
    half = w_query.shape[1] // 2
    heads = half // HD
    place = lax.axis_index("ctx")
    swap = [(index, index ^ 1) for index in range(shards)]
    same_core = [[2 * index + core for index in range(chips)] for core in range(2)]

    def exchange(array):
        return lax.all_to_all(array, "ctx", 0, 0, axis_index_groups=same_core)

    def swapped(array):
        return lax.ppermute(array, "ctx", swap)

    mine = (hidden, w_query, w_key, w_value)
    theirs = tuple(swapped(array) for array in mine)
    packed = jnp.concatenate(mine + (key_cache[: hidden.shape[0]],), axis=1)
    partial, sample_keys = pl.pallas_call(
        project_kernel,
        out_shape=(
            jax.ShapeDtypeStruct((chips, rows, half + HD), jnp.float32),
            jax.ShapeDtypeStruct((HD, HD), jnp.bfloat16),
        ),
        in_specs=[VMEM] * 5,
        out_specs=(VMEM, VMEM),
        compiler_params=KERNEL,
    )(packed, *theirs)
    partial, key_sent, value_sent = lax.optimization_barrier((partial, key_cache, value_cache))
    keys_other = swapped(key_sent)
    values_other = swapped(value_sent)
    pieces = exchange(partial)
    pieces, count_sent, places = lax.optimization_barrier((pieces, block_count, positions))
    count_other = swapped(count_sent)
    query_rows, new_own = pl.pallas_call(
        functools.partial(sum_kernel, half),
        out_shape=(
            jax.ShapeDtypeStruct((chips, rows, half), jnp.bfloat16),
            jax.ShapeDtypeStruct((rows, HD), jnp.bfloat16),
        ),
        in_specs=[VMEM],
        out_specs=(VMEM, VMEM),
        compiler_params=KERNEL,
    )(pieces)
    new_other = swapped(new_own)
    queries = exchange(query_rows).reshape(query_count, half)
    lanes = pltpu.VMEM((heads * query_count, HD), jnp.float32)
    local = pl.pallas_call(
        functools.partial(attend_kernel, heads),
        out_shape=jax.ShapeDtypeStruct((query_count, half + HD), jnp.bfloat16),
        in_specs=[SMEM] * 2 + [VMEM] * 2 + [HBM] * 4 + [VMEM] * 3,
        out_specs=VMEM,
        scratch_shapes=[
            pltpu.VMEM((2 * key_cache.shape[0], HD), jnp.bfloat16),
            pltpu.VMEM((2 * value_cache.shape[0], HD), jnp.bfloat16),
            pltpu.VMEM((HD, HD), jnp.bfloat16),
            pltpu.VMEM((HD, HD), jnp.bfloat16),
            pltpu.VMEM((heads * query_count, 2 * HD), jnp.bfloat16),
            lanes,
            lanes,
            lanes,
            pltpu.SemaphoreType.DMA((4,)),
        ],
        compiler_params=KERNEL,
    )(
        block_count,
        count_other,
        queries,
        sample_keys,
        key_cache,
        value_cache,
        keys_other,
        values_other,
        new_own,
        new_other,
        places.astype(jnp.float32)[None, :],
    )
    groups = exchange(local.reshape(chips, rows, half + HD))
    context_rows = pl.pallas_call(
        functools.partial(combine_kernel, heads),
        out_shape=jax.ShapeDtypeStruct((chips, rows, half), jnp.bfloat16),
        in_specs=[VMEM],
        out_specs=VMEM,
        compiler_params=KERNEL,
    )(groups)
    context = exchange(context_rows).reshape(query_count, half)
    context_other = lax.ppermute(context, "ctx", swap)
    start = (place % 2) * half
    out_own = lax.dynamic_slice_in_dim(w_out, start, half, 0)
    out_other = lax.dynamic_slice_in_dim(w_out, half - start, half, 0)
    attended = jnp.dot(context, out_own, preferred_element_type=jnp.float32) + jnp.dot(
        context_other, out_other, preferred_element_type=jnp.float32
    )
    parts = lax.axis_size("tp")
    attended = attended.astype(jnp.bfloat16).reshape(parts, query_count // parts, -1)
    received = lax.all_to_all(attended, "tp", 0, 0)
    return jnp.sum(received.astype(jnp.float32), axis=0).astype(jnp.bfloat16)


def solution(mesh):
    return jax.shard_map(
        functools.partial(on_device, mesh.shape["ctx"]),
        mesh=mesh,
        in_specs=(
            P(None, "ctx"),
            P("ctx", "tp"),
            P("ctx", "tp"),
            P("ctx", "tp"),
            P("tp", "ctx"),
            P("ctx", "tp"),
            P("ctx", "tp"),
            P("ctx"),
            P(),
        ),
        out_specs=P("tp", "ctx"),
        check_vma=False,
    )
```

```python
import functools

import jax
import jax.numpy as jnp
from jax import lax
from jax.experimental import pallas as pl
from jax.experimental.pallas import tpu as pltpu
from jax.sharding import PartitionSpec as P

H = 64
KVH = 8
HD = 128
SPAN = 2048
CHUNK = 1024
STEP = 512
LOG2E = 1.4426950408889634
LARGE = 2.0**100
SMALL = 2.0**-60
RAISE = 32.0
ROWS_BY_ROWS = (((1,), (1,)), ((), ()))
VMEM = pl.BlockSpec(memory_space=pltpu.VMEM)
SMEM = pl.BlockSpec(memory_space=pltpu.SMEM)
HBM = pl.BlockSpec(memory_space=pltpu.HBM)
KERNEL = pltpu.CompilerParams(vmem_limit_bytes=32 * 2**20)


def core_of():
    return lax.rem(lax.axis_index("ctx"), 2)


def project_kernel(packed, hidden, query, key, value, out, sample):
    sample[...] = packed[:HD, -HD:]
    core = core_of()
    chips, rows, _ = out.shape
    width = query.shape[1]
    half = width // 2
    depth = hidden.shape[1]
    starts = [depth + core * half, depth + width + core * HD]
    own = [
        packed[:, pl.ds(pl.multiple_of(start, HD), size)]
        for start, size in zip(starts, (half, HD))
    ]

    def product(one, two):
        return (
            jnp.dot(packed[:, :depth], one, preferred_element_type=jnp.float32)
            + jnp.dot(hidden[...], two, preferred_element_type=jnp.float32)
        ).reshape(chips, rows, -1)

    columns = pl.ds(pl.multiple_of(core * half, half), half)
    out[:, :, :half] = product(own[0], query[:, columns])
    for index, weights in enumerate((key, value)):

        @pl.when(core == index)
        def _(weights=weights):
            out[:, :, half:] = product(own[1], weights[...])


def spread_kernel(width, sums, queries, other):
    total = sums[...]
    rows = (total[:, :width] * HD ** (-0.5)).astype(jnp.bfloat16)
    for place in range(queries.shape[0]):
        queries[place] = rows
    other[...] = total[:, width:].astype(jnp.bfloat16)


def three_parts(value):
    high = value.astype(jnp.bfloat16).astype(jnp.float32)
    rest = value - high
    middle = rest.astype(jnp.bfloat16).astype(jnp.float32)
    return (high, middle, rest - middle)


def attend_kernel(
    heads, count0, count1, queries, sample_keys, keys0, values0, keys1, values1, new_own,
    new_other, positions, out, keys, values, new_keys, new_values, stacked, reference, total,
    summed, arrivals,
):
    rows = queries.shape[0]
    block = keys0.shape[0]
    fetches = [
        pltpu.make_async_copy(
            source, target.at[pl.ds(index // 2 * block, block)], arrivals.at[index]
        )
        for index, (source, target) in enumerate(
            ((keys0, keys), (values0, values), (keys1, keys), (values1, values))
        )
    ]
    for fetch in fetches[:2]:
        fetch.start()
    lane = lax.broadcasted_iota(jnp.int32, (rows, HD), 1)
    count = new_own.shape[0]
    first = lax.axis_index("ctx") // 2 * count
    offset = lax.rem(first, HD)
    row_positions = jnp.transpose(jnp.broadcast_to(positions[...], (HD, rows)))
    key_positions = positions[:, pl.ds(pl.multiple_of(first - offset, HD), HD)]
    visible = (key_positions <= row_positions) & (lane >= offset) & (lane < offset + count)
    new_keys[...] = jnp.zeros_like(new_keys)
    new_values[...] = jnp.zeros_like(new_values)
    new_at = pl.ds(pl.multiple_of(offset, count), count)
    for index, pair in enumerate(((new_own, new_other), (new_other, new_own))):

        @pl.when(core_of() == index)
        def _(pair=pair):
            new_keys[new_at] = pair[0][...]
            new_values[new_at] = pair[1][...]

    def score(query, key):
        return lax.dot_general(
            query, key, ROWS_BY_ROWS, preferred_element_type=jnp.float32
        )

    sample = jnp.concatenate([sample_keys[...], new_keys[...]], axis=0)
    for head in range(heads):
        at = slice(head * rows, (head + 1) * rows)
        query = queries[:, head * HD : (head + 1) * HD]
        scores = score(query, sample)
        own = jnp.where(visible, scores[:, HD:], -jnp.inf)
        top = jnp.max(jnp.maximum(scores[:, :HD], own), axis=1, keepdims=True)
        level = jnp.broadcast_to(top, (rows, HD)).astype(jnp.bfloat16).astype(jnp.float32)
        stacked[at, :HD] = query
        stacked[at, HD:] = jnp.where(
            lane == 0, -level, jnp.where(lane == 1, 1.0, 0.0)
        ).astype(jnp.bfloat16)
        weights = jnp.exp2((own - level) * LOG2E)
        reference[at] = level
        total[at] = jnp.broadcast_to(jnp.sum(weights, axis=1, keepdims=True), (rows, HD))
        summed[at] = jnp.dot(
            weights.astype(jnp.bfloat16), new_values[...], preferred_element_type=jnp.float32
        )

    for fetch in fetches[2:]:
        fetch.start()
    span_lane = lax.broadcasted_iota(jnp.int32, (SPAN, HD), 1)

    def read_block(which, carry):
        for near in range(2):

            @pl.when(which == near)
            def _(near=near):
                fetches[2 * near].wait()
                fetches[2 * near + 1].wait()

        base = which * block
        limit = jnp.where(which == 0, count0[0], count1[0])

        def read_span(step, carry):
            start = pl.multiple_of(base + step * SPAN, SPAN)
            value = values[pl.ds(start, SPAN), :]
            place = step * SPAN + lax.broadcasted_iota(jnp.int32, (SPAN, HD), 0)
            bias = jnp.where(place < limit, 0.0, -1e30)
            extra = jnp.where(span_lane == 0, 1.0, jnp.where(span_lane == 1, bias, 0.0))
            key = jnp.concatenate(
                [keys[pl.ds(start, SPAN), :], extra.astype(jnp.bfloat16)], axis=1
            )
            for first_row in range(0, heads * rows, CHUNK):
                at = slice(first_row, first_row + CHUNK)
                scores = score(stacked[at], key)
                weights = jnp.exp2(scores * LOG2E)
                total[at] = total[at] + jnp.sum(weights, axis=1, keepdims=True)
                summed[at] = summed[at] + jnp.dot(
                    weights.astype(jnp.bfloat16), value, preferred_element_type=jnp.float32
                )
            return carry

        return lax.fori_loop(0, (limit + SPAN - 1) // SPAN, read_span, carry)

    lax.fori_loop(0, 2, read_block, 0)
    in_range = jnp.logical_and(jnp.max(total[...]) < LARGE, jnp.min(total[...]) > SMALL)

    @pl.when(jnp.logical_not(in_range))
    def _():
        reference[...] = jnp.full_like(reference, -jnp.inf)
        total[...] = jnp.zeros_like(total)
        summed[...] = jnp.zeros_like(summed)

        def update(at, scores, value):
            before = reference[at]
            now = jnp.maximum(before, jnp.max(scores, axis=1, keepdims=True))
            keep = jnp.exp(before - now)
            weights = jnp.exp(scores - now[:, :1])
            total[at] = total[at] * keep + jnp.sum(weights, axis=1, keepdims=True)
            summed[at] = summed[at] * keep + jnp.dot(
                weights.astype(jnp.bfloat16), value, preferred_element_type=jnp.float32
            )
            reference[at] = now

        def query_of(head):
            return queries[:, head * HD : (head + 1) * HD]

        def read_again(which, carry):
            base = which * block
            limit = jnp.where(which == 0, count0[0], count1[0])

            def read_step(step, carry):
                start = pl.multiple_of(base + step * STEP, STEP)
                place = step * STEP + lax.broadcasted_iota(jnp.int32, (1, STEP), 1)
                key = keys[pl.ds(start, STEP), :]
                value = values[pl.ds(start, STEP), :]
                for head in range(heads):
                    scores = jnp.where(place < limit, score(query_of(head), key), -jnp.inf)
                    update(slice(head * rows, (head + 1) * rows), scores, value)
                return carry

            return lax.fori_loop(0, (limit + STEP - 1) // STEP, read_step, carry)

        lax.fori_loop(0, 2, read_again, 0)
        for head in range(heads):
            scores = jnp.where(visible, score(query_of(head), new_keys[...]), -jnp.inf)
            update(slice(head * rows, (head + 1) * rows), scores, new_values[...])

    statistics = jnp.zeros((rows, HD), jnp.float32)
    for head in range(heads):
        at = slice(head * rows, (head + 1) * rows)
        out[:, head * HD : (head + 1) * HD] = summed[at].astype(jnp.bfloat16)
        parts = three_parts(reference[at]) + three_parts(total[at])
        for place, part in enumerate(parts):
            statistics = jnp.where(lane == 8 * head + place, part, statistics)
    out[:, heads * HD :] = statistics.astype(jnp.bfloat16)


def combine_kernel(heads, pieces, out):
    sources, rows, _ = pieces.shape
    width = heads * HD
    statistics = pieces[:, :, width:].reshape(sources * rows, HD)
    place = lax.broadcasted_iota(jnp.int32, (HD, width), 0)
    column = lax.broadcasted_iota(jnp.int32, (HD, width), 1)
    own = place // 8 == column // HD
    pick_top = jnp.where(own & (place % 8 < 3), 1.0, 0.0).astype(jnp.bfloat16)
    pick_total = jnp.where(own & (place % 8 >= 3) & (place % 8 < 6), 1.0, 0.0)
    tops = jnp.dot(statistics, pick_top, preferred_element_type=jnp.float32)
    totals = jnp.dot(
        statistics, pick_total.astype(jnp.bfloat16), preferred_element_type=jnp.float32
    )
    tops = tops.reshape(sources, rows, width)
    totals = totals.reshape(sources, rows, width)
    scale = jnp.exp(tops - jnp.max(tops, axis=0, keepdims=True))
    summed = jnp.sum(scale * pieces[:, :, :width].astype(jnp.float32), axis=0)
    context = (summed / jnp.sum(scale * totals, axis=0)).astype(jnp.bfloat16)
    for target in range(out.shape[0]):
        out[target] = context


def on_device(
    shards, hidden, w_query, w_key, w_value, w_out, key_cache, value_cache, block_count, positions
):
    query_count = hidden.shape[0]
    chips = shards // 2
    rows = query_count // chips
    half = w_query.shape[1] // 2
    heads = half // HD
    place = lax.axis_index("ctx")
    swap = [(index, index ^ 1) for index in range(shards)]
    same_core = [[2 * index + core for index in range(chips)] for core in range(2)]

    def exchange(array):
        return lax.all_to_all(array, "ctx", 0, 0, axis_index_groups=same_core)

    def swapped(array):
        return lax.ppermute(array, "ctx", swap)

    mine = (hidden, w_query, w_key, w_value)
    theirs = tuple(swapped(array) for array in mine)
    packed = jnp.concatenate(mine + (key_cache[: hidden.shape[0]],), axis=1)
    partial, sample_keys = pl.pallas_call(
        project_kernel,
        out_shape=(
            jax.ShapeDtypeStruct((chips, rows, half + HD), jnp.float32),
            jax.ShapeDtypeStruct((HD, HD), jnp.bfloat16),
        ),
        in_specs=[VMEM] * 5,
        out_specs=(VMEM, VMEM),
        compiler_params=KERNEL,
    )(packed, *theirs)
    partial, key_sent, value_sent = lax.optimization_barrier((partial, key_cache, value_cache))
    keys_other = swapped(key_sent)
    values_other = swapped(value_sent)
    pieces = exchange((partial * RAISE).astype(jnp.float16))
    pieces, count_sent, places = lax.optimization_barrier((pieces, block_count, positions))
    count_other = swapped(count_sent)
    query_rows, new_own = pl.pallas_call(
        functools.partial(spread_kernel, half),
        out_shape=(
            jax.ShapeDtypeStruct((chips, rows, half), jnp.bfloat16),
            jax.ShapeDtypeStruct((rows, HD), jnp.bfloat16),
        ),
        in_specs=[VMEM],
        out_specs=(VMEM, VMEM),
        compiler_params=KERNEL,
    )(jnp.sum(pieces.astype(jnp.float32), axis=0) * (1.0 / RAISE))
    new_other = swapped(new_own)
    queries = exchange(query_rows).reshape(query_count, half)
    lanes = pltpu.VMEM((heads * query_count, HD), jnp.float32)
    local = pl.pallas_call(
        functools.partial(attend_kernel, heads),
        out_shape=jax.ShapeDtypeStruct((query_count, half + HD), jnp.bfloat16),
        in_specs=[SMEM] * 2 + [VMEM] * 2 + [HBM] * 4 + [VMEM] * 3,
        out_specs=VMEM,
        scratch_shapes=[
            pltpu.VMEM((2 * key_cache.shape[0], HD), jnp.bfloat16),
            pltpu.VMEM((2 * value_cache.shape[0], HD), jnp.bfloat16),
            pltpu.VMEM((HD, HD), jnp.bfloat16),
            pltpu.VMEM((HD, HD), jnp.bfloat16),
            pltpu.VMEM((heads * query_count, 2 * HD), jnp.bfloat16),
            lanes,
            lanes,
            lanes,
            pltpu.SemaphoreType.DMA((4,)),
        ],
        compiler_params=KERNEL,
    )(
        block_count,
        count_other,
        queries,
        sample_keys,
        key_cache,
        value_cache,
        keys_other,
        values_other,
        new_own,
        new_other,
        places.astype(jnp.float32)[None, :],
    )
    groups = exchange(local.reshape(chips, rows, half + HD))
    context_rows = pl.pallas_call(
        functools.partial(combine_kernel, heads),
        out_shape=jax.ShapeDtypeStruct((chips, rows, half), jnp.bfloat16),
        in_specs=[VMEM],
        out_specs=VMEM,
        compiler_params=KERNEL,
    )(groups)
    context = exchange(context_rows).reshape(query_count, half)
    context_other = lax.ppermute(context, "ctx", swap)
    start = (place % 2) * half
    out_own = lax.dynamic_slice_in_dim(w_out, start, half, 0)
    out_other = lax.dynamic_slice_in_dim(w_out, half - start, half, 0)
    attended = jnp.dot(context, out_own, preferred_element_type=jnp.float32) + jnp.dot(
        context_other, out_other, preferred_element_type=jnp.float32
    )
    parts = lax.axis_size("tp")
    attended = attended.astype(jnp.bfloat16).reshape(parts, query_count // parts, -1)
    received = lax.all_to_all(attended, "tp", 0, 0)
    return jnp.sum(received.astype(jnp.float32), axis=0).astype(jnp.bfloat16)


def solution(mesh):
    return jax.shard_map(
        functools.partial(on_device, mesh.shape["ctx"]),
        mesh=mesh,
        in_specs=(
            P(None, "ctx"),
            P("ctx", "tp"),
            P("ctx", "tp"),
            P("ctx", "tp"),
            P("tp", "ctx"),
            P("ctx", "tp"),
            P("ctx", "tp"),
            P("ctx"),
            P(),
        ),
        out_specs=P("tp", "ctx"),
        check_vma=False,
    )
```

```python
import functools

import jax
import jax.numpy as jnp
from jax import lax
from jax.experimental import pallas as pl
from jax.experimental.pallas import tpu as pltpu
from jax.sharding import PartitionSpec as P

H = 64
KVH = 8
HD = 128
SPAN = 2048
CHUNK = 1024
STEP = 512
LOG2E = 1.4426950408889634
LARGE = 2.0**100
SMALL = 2.0**-60
RAISE = 32.0
ROWS_BY_ROWS = (((1,), (1,)), ((), ()))
VMEM = pl.BlockSpec(memory_space=pltpu.VMEM)
SMEM = pl.BlockSpec(memory_space=pltpu.SMEM)
HBM = pl.BlockSpec(memory_space=pltpu.HBM)
KERNEL = pltpu.CompilerParams(vmem_limit_bytes=32 * 2**20)


def core_of():
    return lax.rem(lax.axis_index("ctx"), 2)


def project_kernel(hidden_own, packed, hidden, query, key, value, out):
    core = core_of()
    chips, rows, _ = out.shape
    width = query.shape[1]
    half = width // 2
    starts = [core * half, width + core * HD]
    own = [
        packed[:, pl.ds(pl.multiple_of(start, HD), size)]
        for start, size in zip(starts, (half, HD))
    ]

    def product(one, two):
        return (
            jnp.dot(hidden_own[...], one, preferred_element_type=jnp.float32)
            + jnp.dot(hidden[...], two, preferred_element_type=jnp.float32)
        ).reshape(chips, rows, -1)

    columns = pl.ds(pl.multiple_of(core * half, half), half)
    out[:, :, :half] = product(own[0], query[:, columns])
    for index, weights in enumerate((key, value)):

        @pl.when(core == index)
        def _(weights=weights):
            out[:, :, half:] = product(own[1], weights[...])


def spread_kernel(width, sums, queries, other):
    total = sums[...]
    rows = (total[:, :width] * HD ** (-0.5)).astype(jnp.bfloat16)
    for place in range(queries.shape[0]):
        queries[place] = rows
    other[...] = total[:, width:].astype(jnp.bfloat16)


def three_parts(value):
    high = value.astype(jnp.bfloat16).astype(jnp.float32)
    rest = value - high
    middle = rest.astype(jnp.bfloat16).astype(jnp.float32)
    return (high, middle, rest - middle)


def attend_kernel(
    heads, count0, count1, queries, sample_keys, keys0, values0, keys1, values1, new_own,
    new_other, positions, out, keys, values, new_keys, new_values, stacked, reference, total,
    summed, arrivals,
):
    rows = queries.shape[0]
    block = keys0.shape[0]
    fetches = [
        pltpu.make_async_copy(
            source, target.at[pl.ds(index // 2 * block, block)], arrivals.at[index]
        )
        for index, (source, target) in enumerate(
            ((keys0, keys), (values0, values), (keys1, keys), (values1, values))
        )
    ]
    for fetch in fetches[:2]:
        fetch.start()
    lane = lax.broadcasted_iota(jnp.int32, (rows, HD), 1)
    count = new_own.shape[0]
    first = lax.axis_index("ctx") // 2 * count
    offset = lax.rem(first, HD)
    row_positions = jnp.transpose(jnp.broadcast_to(positions[...], (HD, rows)))
    key_positions = positions[:, pl.ds(pl.multiple_of(first - offset, HD), HD)]
    visible = (key_positions <= row_positions) & (lane >= offset) & (lane < offset + count)
    new_keys[...] = jnp.zeros_like(new_keys)
    new_values[...] = jnp.zeros_like(new_values)
    new_at = pl.ds(pl.multiple_of(offset, count), count)
    for index, pair in enumerate(((new_own, new_other), (new_other, new_own))):

        @pl.when(core_of() == index)
        def _(pair=pair):
            new_keys[new_at] = pair[0][...]
            new_values[new_at] = pair[1][...]

    def score(query, key):
        return lax.dot_general(
            query, key, ROWS_BY_ROWS, preferred_element_type=jnp.float32
        )

    sample = jnp.concatenate([sample_keys[...], new_keys[...]], axis=0)
    for head in range(heads):
        at = slice(head * rows, (head + 1) * rows)
        query = queries[:, head * HD : (head + 1) * HD]
        scores = score(query, sample)
        own = jnp.where(visible, scores[:, HD:], -jnp.inf)
        top = jnp.max(jnp.maximum(scores[:, :HD], own), axis=1, keepdims=True)
        level = jnp.broadcast_to(top, (rows, HD)).astype(jnp.bfloat16).astype(jnp.float32)
        stacked[at, :HD] = query
        stacked[at, HD:] = jnp.where(
            lane == 0, -level, jnp.where(lane == 1, 1.0, 0.0)
        ).astype(jnp.bfloat16)
        weights = jnp.exp2((own - level) * LOG2E)
        reference[at] = level
        total[at] = jnp.broadcast_to(jnp.sum(weights, axis=1, keepdims=True), (rows, HD))
        summed[at] = jnp.dot(
            weights.astype(jnp.bfloat16), new_values[...], preferred_element_type=jnp.float32
        )

    for fetch in fetches[2:]:
        fetch.start()
    span_lane = lax.broadcasted_iota(jnp.int32, (SPAN, HD), 1)

    def read_block(which, carry):
        for near in range(2):

            @pl.when(which == near)
            def _(near=near):
                fetches[2 * near].wait()
                fetches[2 * near + 1].wait()

        base = which * block
        limit = jnp.where(which == 0, count0[0], count1[0])

        def read_span(step, carry):
            start = pl.multiple_of(base + step * SPAN, SPAN)
            value = values[pl.ds(start, SPAN), :]
            place = step * SPAN + lax.broadcasted_iota(jnp.int32, (SPAN, HD), 0)
            bias = jnp.where(place < limit, 0.0, -1e30)
            extra = jnp.where(span_lane == 0, 1.0, jnp.where(span_lane == 1, bias, 0.0))
            key = jnp.concatenate(
                [keys[pl.ds(start, SPAN), :], extra.astype(jnp.bfloat16)], axis=1
            )
            for first_row in range(0, heads * rows, CHUNK):
                at = slice(first_row, first_row + CHUNK)
                scores = score(stacked[at], key)
                weights = jnp.exp2(scores * LOG2E)
                total[at] = total[at] + jnp.sum(weights, axis=1, keepdims=True)
                summed[at] = summed[at] + jnp.dot(
                    weights.astype(jnp.bfloat16), value, preferred_element_type=jnp.float32
                )
            return carry

        return lax.fori_loop(0, (limit + SPAN - 1) // SPAN, read_span, carry)

    lax.fori_loop(0, 2, read_block, 0)
    in_range = jnp.logical_and(jnp.max(total[...]) < LARGE, jnp.min(total[...]) > SMALL)

    @pl.when(jnp.logical_not(in_range))
    def _():
        reference[...] = jnp.full_like(reference, -jnp.inf)
        total[...] = jnp.zeros_like(total)
        summed[...] = jnp.zeros_like(summed)

        def update(at, scores, value):
            before = reference[at]
            now = jnp.maximum(before, jnp.max(scores, axis=1, keepdims=True))
            keep = jnp.exp(before - now)
            weights = jnp.exp(scores - now[:, :1])
            total[at] = total[at] * keep + jnp.sum(weights, axis=1, keepdims=True)
            summed[at] = summed[at] * keep + jnp.dot(
                weights.astype(jnp.bfloat16), value, preferred_element_type=jnp.float32
            )
            reference[at] = now

        def query_of(head):
            return queries[:, head * HD : (head + 1) * HD]

        def read_again(which, carry):
            base = which * block
            limit = jnp.where(which == 0, count0[0], count1[0])

            def read_step(step, carry):
                start = pl.multiple_of(base + step * STEP, STEP)
                place = step * STEP + lax.broadcasted_iota(jnp.int32, (1, STEP), 1)
                key = keys[pl.ds(start, STEP), :]
                value = values[pl.ds(start, STEP), :]
                for head in range(heads):
                    scores = jnp.where(place < limit, score(query_of(head), key), -jnp.inf)
                    update(slice(head * rows, (head + 1) * rows), scores, value)
                return carry

            return lax.fori_loop(0, (limit + STEP - 1) // STEP, read_step, carry)

        lax.fori_loop(0, 2, read_again, 0)
        for head in range(heads):
            scores = jnp.where(visible, score(query_of(head), new_keys[...]), -jnp.inf)
            update(slice(head * rows, (head + 1) * rows), scores, new_values[...])

    statistics = jnp.zeros((rows, HD), jnp.float32)
    for head in range(heads):
        at = slice(head * rows, (head + 1) * rows)
        out[:, head * HD : (head + 1) * HD] = summed[at].astype(jnp.bfloat16)
        parts = three_parts(reference[at]) + three_parts(total[at])
        for place, part in enumerate(parts):
            statistics = jnp.where(lane == 8 * head + place, part, statistics)
    out[:, heads * HD :] = statistics.astype(jnp.bfloat16)


def combine_kernel(heads, pieces, out):
    sources, rows, _ = pieces.shape
    width = heads * HD
    statistics = pieces[:, :, width:].reshape(sources * rows, HD)
    place = lax.broadcasted_iota(jnp.int32, (HD, width), 0)
    column = lax.broadcasted_iota(jnp.int32, (HD, width), 1)
    own = place // 8 == column // HD
    pick_top = jnp.where(own & (place % 8 < 3), 1.0, 0.0).astype(jnp.bfloat16)
    pick_total = jnp.where(own & (place % 8 >= 3) & (place % 8 < 6), 1.0, 0.0)
    tops = jnp.dot(statistics, pick_top, preferred_element_type=jnp.float32)
    totals = jnp.dot(
        statistics, pick_total.astype(jnp.bfloat16), preferred_element_type=jnp.float32
    )
    tops = tops.reshape(sources, rows, width)
    totals = totals.reshape(sources, rows, width)
    scale = jnp.exp(tops - jnp.max(tops, axis=0, keepdims=True))
    summed = jnp.sum(scale * pieces[:, :, :width].astype(jnp.float32), axis=0)
    context = (summed / jnp.sum(scale * totals, axis=0)).astype(jnp.bfloat16)
    for target in range(out.shape[0]):
        out[target] = context


def on_device(
    shards, hidden, w_query, w_key, w_value, w_out, key_cache, value_cache, block_count, positions
):
    query_count = hidden.shape[0]
    chips = shards // 2
    rows = query_count // chips
    half = w_query.shape[1] // 2
    heads = half // HD
    place = lax.axis_index("ctx")
    swap = [(index, index ^ 1) for index in range(shards)]
    same_core = [[2 * index + core for index in range(chips)] for core in range(2)]

    def exchange(array):
        return lax.all_to_all(array, "ctx", 0, 0, axis_index_groups=same_core)

    def swapped(array):
        return lax.ppermute(array, "ctx", swap)

    mine = (hidden, w_query, w_key, w_value)
    theirs = tuple(swapped(array) for array in mine)
    packed = jnp.concatenate(mine[1:], axis=1)
    partial = pl.pallas_call(
        project_kernel,
        out_shape=jax.ShapeDtypeStruct((chips, rows, half + HD), jnp.float32),
        in_specs=[VMEM] * 6,
        out_specs=VMEM,
        compiler_params=KERNEL,
    )(hidden, packed, *theirs)
    pieces = exchange((partial * RAISE).astype(jnp.float16))
    pieces, count_sent, places = lax.optimization_barrier((pieces, block_count, positions))
    count_other = swapped(count_sent)
    query_rows, new_own = pl.pallas_call(
        functools.partial(spread_kernel, half),
        out_shape=(
            jax.ShapeDtypeStruct((chips, rows, half), jnp.bfloat16),
            jax.ShapeDtypeStruct((rows, HD), jnp.bfloat16),
        ),
        in_specs=[VMEM],
        out_specs=(VMEM, VMEM),
        compiler_params=KERNEL,
    )(jnp.sum(pieces.astype(jnp.float32), axis=0) * (1.0 / RAISE))
    new_own, key_sent, value_sent = lax.optimization_barrier((new_own, key_cache, value_cache))
    sample_keys = key_sent[:HD]
    keys_other = swapped(key_sent)
    values_other = swapped(value_sent)
    new_other = swapped(new_own)
    queries = exchange(query_rows).reshape(query_count, half)
    lanes = pltpu.VMEM((heads * query_count, HD), jnp.float32)
    local = pl.pallas_call(
        functools.partial(attend_kernel, heads),
        out_shape=jax.ShapeDtypeStruct((query_count, half + HD), jnp.bfloat16),
        in_specs=[SMEM] * 2 + [VMEM] * 2 + [HBM] * 4 + [VMEM] * 3,
        out_specs=VMEM,
        scratch_shapes=[
            pltpu.VMEM((2 * key_cache.shape[0], HD), jnp.bfloat16),
            pltpu.VMEM((2 * value_cache.shape[0], HD), jnp.bfloat16),
            pltpu.VMEM((HD, HD), jnp.bfloat16),
            pltpu.VMEM((HD, HD), jnp.bfloat16),
            pltpu.VMEM((heads * query_count, 2 * HD), jnp.bfloat16),
            lanes,
            lanes,
            lanes,
            pltpu.SemaphoreType.DMA((4,)),
        ],
        compiler_params=KERNEL,
    )(
        block_count,
        count_other,
        queries,
        sample_keys,
        key_cache,
        value_cache,
        keys_other,
        values_other,
        new_own,
        new_other,
        places.astype(jnp.float32)[None, :],
    )
    groups = exchange(local.reshape(chips, rows, half + HD))
    context_rows = pl.pallas_call(
        functools.partial(combine_kernel, heads),
        out_shape=jax.ShapeDtypeStruct((chips, rows, half), jnp.bfloat16),
        in_specs=[VMEM],
        out_specs=VMEM,
        compiler_params=KERNEL,
    )(groups)
    context = exchange(context_rows).reshape(query_count, half)
    context_other = lax.ppermute(context, "ctx", swap)
    start = (place % 2) * half
    out_own = lax.dynamic_slice_in_dim(w_out, start, half, 0)
    out_other = lax.dynamic_slice_in_dim(w_out, half - start, half, 0)
    attended = jnp.dot(context, out_own, preferred_element_type=jnp.float32) + jnp.dot(
        context_other, out_other, preferred_element_type=jnp.float32
    )
    parts = lax.axis_size("tp")
    attended = attended.astype(jnp.bfloat16).reshape(parts, query_count // parts, -1)
    received = lax.all_to_all(attended, "tp", 0, 0)
    return jnp.sum(received.astype(jnp.float32), axis=0).astype(jnp.bfloat16)


def solution(mesh):
    return jax.shard_map(
        functools.partial(on_device, mesh.shape["ctx"]),
        mesh=mesh,
        in_specs=(
            P(None, "ctx"),
            P("ctx", "tp"),
            P("ctx", "tp"),
            P("ctx", "tp"),
            P("tp", "ctx"),
            P("ctx", "tp"),
            P("ctx", "tp"),
            P("ctx"),
            P(),
        ),
        out_specs=P("tp", "ctx"),
        check_vma=False,
    )
```

```python
import functools

import jax
import jax.numpy as jnp
from jax import lax
from jax.experimental import pallas as pl
from jax.experimental.pallas import tpu as pltpu
from jax.sharding import PartitionSpec as P

H = 64
KVH = 8
HD = 128
SPAN = 2048
CHUNK = 1024
STEP = 512
LOG2E = 1.4426950408889634
LARGE = 2.0**100
SMALL = 2.0**-60
RAISE = 32.0
ROWS_BY_ROWS = (((1,), (1,)), ((), ()))
VMEM = pl.BlockSpec(memory_space=pltpu.VMEM)
SMEM = pl.BlockSpec(memory_space=pltpu.SMEM)
HBM = pl.BlockSpec(memory_space=pltpu.HBM)
KERNEL = pltpu.CompilerParams(vmem_limit_bytes=32 * 2**20)


def core_of():
    return lax.rem(lax.axis_index("ctx"), 2)


def project_kernel(hidden_own, packed, hidden, query, key, value, out):
    core = core_of()
    chips, rows, _ = out.shape
    width = query.shape[1]
    half = width // 2
    starts = [core * half, width + core * HD]
    own = [
        packed[:, pl.ds(pl.multiple_of(start, HD), size)]
        for start, size in zip(starts, (half, HD))
    ]

    def product(one, two):
        return (
            jnp.dot(hidden_own[...], one, preferred_element_type=jnp.float32)
            + jnp.dot(hidden[...], two, preferred_element_type=jnp.float32)
        ).reshape(chips, rows, -1)

    columns = pl.ds(pl.multiple_of(core * half, half), half)
    out[:, :, :half] = product(own[0], query[:, columns])
    for index, weights in enumerate((key, value)):

        @pl.when(core == index)
        def _(weights=weights):
            out[:, :, half:] = product(own[1], weights[...])


def spread_kernel(width, sums, queries, other):
    total = sums[...]
    rows = (total[:, :width] * HD ** (-0.5)).astype(jnp.bfloat16)
    for place in range(queries.shape[0]):
        queries[place] = rows
    other[...] = total[:, width:].astype(jnp.bfloat16)


def three_parts(value):
    high = value.astype(jnp.bfloat16).astype(jnp.float32)
    rest = value - high
    middle = rest.astype(jnp.bfloat16).astype(jnp.float32)
    return (high, middle, rest - middle)


def attend_kernel(
    heads, count0, count1, queries, sample_keys, keys0, values0, keys1, values1, new_own,
    new_other, positions, out, keys, values, new_keys, new_values, stacked, reference, total,
    summed, arrivals,
):
    rows = queries.shape[0]
    block = keys0.shape[0]
    fetches = [
        pltpu.make_async_copy(
            source, target.at[pl.ds(index // 2 * block, block)], arrivals.at[index]
        )
        for index, (source, target) in enumerate(
            ((keys0, keys), (values0, values), (keys1, keys), (values1, values))
        )
    ]
    for fetch in fetches[:2]:
        fetch.start()
    lane = lax.broadcasted_iota(jnp.int32, (rows, HD), 1)
    count = new_own.shape[0]
    first = lax.axis_index("ctx") // 2 * count
    offset = lax.rem(first, HD)
    row_positions = jnp.transpose(jnp.broadcast_to(positions[...], (HD, rows)))
    key_positions = positions[:, pl.ds(pl.multiple_of(first - offset, HD), HD)]
    visible = (key_positions <= row_positions) & (lane >= offset) & (lane < offset + count)
    new_keys[...] = jnp.zeros_like(new_keys)
    new_values[...] = jnp.zeros_like(new_values)
    new_at = pl.ds(pl.multiple_of(offset, count), count)
    for index, pair in enumerate(((new_own, new_other), (new_other, new_own))):

        @pl.when(core_of() == index)
        def _(pair=pair):
            new_keys[new_at] = pair[0][...]
            new_values[new_at] = pair[1][...]

    def score(query, key):
        return lax.dot_general(
            query, key, ROWS_BY_ROWS, preferred_element_type=jnp.float32
        )

    sample = jnp.concatenate([sample_keys[...], new_keys[...]], axis=0)
    for head in range(heads):
        at = slice(head * rows, (head + 1) * rows)
        query = queries[:, head * HD : (head + 1) * HD]
        scores = score(query, sample)
        own = jnp.where(visible, scores[:, HD:], -jnp.inf)
        top = jnp.max(jnp.maximum(scores[:, :HD], own), axis=1, keepdims=True)
        level = jnp.broadcast_to(top, (rows, HD)).astype(jnp.bfloat16).astype(jnp.float32)
        stacked[at, :HD] = query
        stacked[at, HD:] = jnp.where(
            lane == 0, -level, jnp.where(lane == 1, 1.0, 0.0)
        ).astype(jnp.bfloat16)
        weights = jnp.exp2((own - level) * LOG2E)
        reference[at] = level
        total[at] = jnp.broadcast_to(jnp.sum(weights, axis=1, keepdims=True), (rows, HD))
        summed[at] = jnp.dot(
            weights.astype(jnp.bfloat16), new_values[...], preferred_element_type=jnp.float32
        )

    for fetch in fetches[2:]:
        fetch.start()
    span_lane = lax.broadcasted_iota(jnp.int32, (SPAN, HD), 1)

    def read_block(which, carry):
        for near in range(2):

            @pl.when(which == near)
            def _(near=near):
                fetches[2 * near].wait()
                fetches[2 * near + 1].wait()

        base = which * block
        limit = jnp.where(which == 0, count0[0], count1[0])

        def read_span(step, carry):
            start = pl.multiple_of(base + step * SPAN, SPAN)
            value = values[pl.ds(start, SPAN), :]
            place = step * SPAN + lax.broadcasted_iota(jnp.int32, (SPAN, HD), 0)
            bias = jnp.where(place < limit, 0.0, -1e30)
            extra = jnp.where(span_lane == 0, 1.0, jnp.where(span_lane == 1, bias, 0.0))
            key = jnp.concatenate(
                [keys[pl.ds(start, SPAN), :], extra.astype(jnp.bfloat16)], axis=1
            )
            for first_row in range(0, heads * rows, CHUNK):
                at = slice(first_row, first_row + CHUNK)
                scores = score(stacked[at], key)
                weights = jnp.exp2(scores * LOG2E)
                total[at] = total[at] + jnp.sum(weights, axis=1, keepdims=True)
                summed[at] = summed[at] + jnp.dot(
                    weights.astype(jnp.bfloat16), value, preferred_element_type=jnp.float32
                )
            return carry

        return lax.fori_loop(0, (limit + SPAN - 1) // SPAN, read_span, carry)

    lax.fori_loop(0, 2, read_block, 0)
    in_range = jnp.logical_and(jnp.max(total[...]) < LARGE, jnp.min(total[...]) > SMALL)

    @pl.when(jnp.logical_not(in_range))
    def _():
        reference[...] = jnp.full_like(reference, -jnp.inf)
        total[...] = jnp.zeros_like(total)
        summed[...] = jnp.zeros_like(summed)

        def update(at, scores, value):
            before = reference[at]
            now = jnp.maximum(before, jnp.max(scores, axis=1, keepdims=True))
            keep = jnp.exp(before - now)
            weights = jnp.exp(scores - now[:, :1])
            total[at] = total[at] * keep + jnp.sum(weights, axis=1, keepdims=True)
            summed[at] = summed[at] * keep + jnp.dot(
                weights.astype(jnp.bfloat16), value, preferred_element_type=jnp.float32
            )
            reference[at] = now

        def query_of(head):
            return queries[:, head * HD : (head + 1) * HD]

        def read_again(which, carry):
            base = which * block
            limit = jnp.where(which == 0, count0[0], count1[0])

            def read_step(step, carry):
                start = pl.multiple_of(base + step * STEP, STEP)
                place = step * STEP + lax.broadcasted_iota(jnp.int32, (1, STEP), 1)
                key = keys[pl.ds(start, STEP), :]
                value = values[pl.ds(start, STEP), :]
                for head in range(heads):
                    scores = jnp.where(place < limit, score(query_of(head), key), -jnp.inf)
                    update(slice(head * rows, (head + 1) * rows), scores, value)
                return carry

            return lax.fori_loop(0, (limit + STEP - 1) // STEP, read_step, carry)

        lax.fori_loop(0, 2, read_again, 0)
        for head in range(heads):
            scores = jnp.where(visible, score(query_of(head), new_keys[...]), -jnp.inf)
            update(slice(head * rows, (head + 1) * rows), scores, new_values[...])

    statistics = jnp.zeros((rows, HD), jnp.float32)
    for head in range(heads):
        at = slice(head * rows, (head + 1) * rows)
        out[:, head * HD : (head + 1) * HD] = summed[at].astype(jnp.bfloat16)
        parts = three_parts(reference[at]) + three_parts(total[at])
        for place, part in enumerate(parts):
            statistics = jnp.where(lane == 8 * head + place, part, statistics)
    out[:, heads * HD :] = statistics.astype(jnp.bfloat16)


def combine_kernel(heads, pieces, out):
    sources, rows, _ = pieces.shape
    width = heads * HD
    statistics = pieces[:, :, width:].reshape(sources * rows, HD)
    place = lax.broadcasted_iota(jnp.int32, (HD, width), 0)
    column = lax.broadcasted_iota(jnp.int32, (HD, width), 1)
    own = place // 8 == column // HD
    pick_top = jnp.where(own & (place % 8 < 3), 1.0, 0.0).astype(jnp.bfloat16)
    pick_total = jnp.where(own & (place % 8 >= 3) & (place % 8 < 6), 1.0, 0.0)
    tops = jnp.dot(statistics, pick_top, preferred_element_type=jnp.float32)
    totals = jnp.dot(
        statistics, pick_total.astype(jnp.bfloat16), preferred_element_type=jnp.float32
    )
    tops = tops.reshape(sources, rows, width)
    totals = totals.reshape(sources, rows, width)
    scale = jnp.exp(tops - jnp.max(tops, axis=0, keepdims=True))
    summed = jnp.sum(scale * pieces[:, :, :width].astype(jnp.float32), axis=0)
    context = (summed / jnp.sum(scale * totals, axis=0)).astype(jnp.bfloat16)
    for target in range(out.shape[0]):
        out[target] = context


def total_kernel(pieces, out):
    out[...] = jnp.sum(pieces[...].astype(jnp.float32), axis=0).astype(jnp.bfloat16)


def on_device(
    shards, hidden, w_query, w_key, w_value, w_out, key_cache, value_cache, block_count, positions
):
    query_count = hidden.shape[0]
    chips = shards // 2
    rows = query_count // chips
    half = w_query.shape[1] // 2
    heads = half // HD
    place = lax.axis_index("ctx")
    swap = [(index, index ^ 1) for index in range(shards)]
    same_core = [[2 * index + core for index in range(chips)] for core in range(2)]

    def exchange(array):
        return lax.all_to_all(array, "ctx", 0, 0, axis_index_groups=same_core)

    def swapped(array):
        return lax.ppermute(array, "ctx", swap)

    mine = (hidden, w_query, w_key, w_value)
    theirs = tuple(swapped(array) for array in mine)
    packed = jnp.concatenate(mine[1:], axis=1)
    partial = pl.pallas_call(
        project_kernel,
        out_shape=jax.ShapeDtypeStruct((chips, rows, half + HD), jnp.float32),
        in_specs=[VMEM] * 6,
        out_specs=VMEM,
        compiler_params=KERNEL,
    )(hidden, packed, *theirs)
    pieces = exchange((partial * RAISE).astype(jnp.float16))
    pieces, count_sent, places = lax.optimization_barrier((pieces, block_count, positions))
    count_other = swapped(count_sent)
    query_rows, new_own = pl.pallas_call(
        functools.partial(spread_kernel, half),
        out_shape=(
            jax.ShapeDtypeStruct((chips, rows, half), jnp.bfloat16),
            jax.ShapeDtypeStruct((rows, HD), jnp.bfloat16),
        ),
        in_specs=[VMEM],
        out_specs=(VMEM, VMEM),
        compiler_params=KERNEL,
    )(jnp.sum(pieces.astype(jnp.float32), axis=0) * (1.0 / RAISE))
    new_own, key_sent, value_sent = lax.optimization_barrier((new_own, key_cache, value_cache))
    sample_keys = key_sent[:HD]
    keys_other = swapped(key_sent)
    values_other = swapped(value_sent)
    new_other = swapped(new_own)
    queries = exchange(query_rows).reshape(query_count, half)
    lanes = pltpu.VMEM((heads * query_count, HD), jnp.float32)
    local = pl.pallas_call(
        functools.partial(attend_kernel, heads),
        out_shape=jax.ShapeDtypeStruct((query_count, half + HD), jnp.bfloat16),
        in_specs=[SMEM] * 2 + [VMEM] * 2 + [HBM] * 4 + [VMEM] * 3,
        out_specs=VMEM,
        scratch_shapes=[
            pltpu.VMEM((2 * key_cache.shape[0], HD), jnp.bfloat16),
            pltpu.VMEM((2 * value_cache.shape[0], HD), jnp.bfloat16),
            pltpu.VMEM((HD, HD), jnp.bfloat16),
            pltpu.VMEM((HD, HD), jnp.bfloat16),
            pltpu.VMEM((heads * query_count, 2 * HD), jnp.bfloat16),
            lanes,
            lanes,
            lanes,
            pltpu.SemaphoreType.DMA((4,)),
        ],
        compiler_params=KERNEL,
    )(
        block_count,
        count_other,
        queries,
        sample_keys,
        key_cache,
        value_cache,
        keys_other,
        values_other,
        new_own,
        new_other,
        places.astype(jnp.float32)[None, :],
    )
    groups = exchange(local.reshape(chips, rows, half + HD))
    context_rows = pl.pallas_call(
        functools.partial(combine_kernel, heads),
        out_shape=jax.ShapeDtypeStruct((chips, rows, half), jnp.bfloat16),
        in_specs=[VMEM],
        out_specs=VMEM,
        compiler_params=KERNEL,
    )(groups)
    context = exchange(context_rows).reshape(query_count, half)
    context_other = lax.ppermute(context, "ctx", swap)
    start = (place % 2) * half
    out_own = lax.dynamic_slice_in_dim(w_out, start, half, 0)
    out_other = lax.dynamic_slice_in_dim(w_out, half - start, half, 0)
    attended = jnp.dot(context, out_own, preferred_element_type=jnp.float32) + jnp.dot(
        context_other, out_other, preferred_element_type=jnp.float32
    )
    parts = lax.axis_size("tp")
    attended = attended.astype(jnp.bfloat16).reshape(parts, query_count // parts, -1)
    received = lax.all_to_all(attended, "tp", 0, 0)
    return pl.pallas_call(
        total_kernel,
        out_shape=jax.ShapeDtypeStruct(received.shape[1:], jnp.bfloat16),
        in_specs=[VMEM],
        out_specs=VMEM,
        compiler_params=KERNEL,
    )(received)


def solution(mesh):
    return jax.shard_map(
        functools.partial(on_device, mesh.shape["ctx"]),
        mesh=mesh,
        in_specs=(
            P(None, "ctx"),
            P("ctx", "tp"),
            P("ctx", "tp"),
            P("ctx", "tp"),
            P("tp", "ctx"),
            P("ctx", "tp"),
            P("ctx", "tp"),
            P("ctx"),
            P(),
        ),
        out_specs=P("tp", "ctx"),
        check_vma=False,
    )
```
